32 devices in a mesh: rows: 8 (over z, x), sub: 4 (over y, core).
Axes of the slice: x: 2, y: 2, z: 4, core: 2. Of those that a mesh axis runs over, the one named last changes fastest.
Arguments:
- documents: bfloat16 [65536, 1024], P(('rows', 'sub')), may hold values from -40 to 40
- centroids: bfloat16 [1024, 1024], replicated, may hold values from -5 to 5
- cluster_mass: float32 [1024], replicated, may hold values from 0.00024414062 to 0.00390625
Outputs:
- new_centroids: bfloat16 [1024, 1024], P('sub')
- cluster_duals: float32 [1024], replicated
The draws below stay inside these ranges and needn't reach their ends.
All inputs are finite; a program needn't handle non-finite values.
Results may differ from the reference program's by a relative error of at most 0.0038.
Values may be sent and summed in bfloat16 or wider, within the bound.
A program may use at most 64 MiB of HBM per device.

```python
import math
import jax
import jax.numpy as jnp
from jax import lax

D = 1024
K = 1024
ITERS = 3
NDOC = 65536


def base_centroids(key):
    inner = jax.random.fold_in(key, 11)
    values = jax.random.normal(inner, (K, D), jnp.float32)
    return jnp.clip(values, -5.0, 5.0)


def draw_centroids(key, part):
    return base_centroids(key).astype(jnp.bfloat16)


def draw_documents(key, part):
    cent = base_centroids(key)
    index = jnp.arange(NDOC)
    spread_rows = (index * 7 % 16 < 7)[:, None]
    cluster = index * K // NDOC
    noise = jax.random.normal(jax.random.fold_in(key, 23), (NDOC, D), jnp.float32)
    common = jax.random.normal(jax.random.fold_in(key, 22), (1, D), jnp.float32)
    common_weight = 0.25
    amplitude = 3.2 / math.sqrt(D)
    core = amplitude * cent[cluster] + 0.3 * noise
    diffuse = 0.4 * noise + common_weight * common
    values = jnp.where(spread_rows, diffuse, core)
    return jnp.clip(values, -40.0, 40.0).astype(jnp.bfloat16)


def setup_inputs(seed: int = 0) -> dict:
    keys = jax.random.split(jax.random.key(seed), 4)
    documents = draw_documents(jax.random.fold_in(keys[3], 71), 0)
    centroids = draw_centroids(jax.random.fold_in(keys[3], 71), 0)
    cluster_mass = jnp.clip(jnp.exp(jax.random.uniform(keys[2], (K,), jnp.float32, math.log(0.00024414062), math.log(0.00390625))), 0.00024414062, 0.00390625)
    return {"documents": documents, "centroids": centroids, "cluster_mass": cluster_mass}


TAU = 0.8
TEMP = 4.0

def reference(documents, centroids, cluster_mass):
    scores = lax.dot_general(documents, centroids, (((1,), (1,)), ((), ())), preferred_element_type=jnp.float32) * (TEMP / math.sqrt(D))
    loga = -jnp.log(jnp.asarray(NDOC, jnp.float32))
    duals = jnp.zeros((K,), jnp.float32)
    for step in range(ITERS):
        lse = jax.nn.logsumexp(scores + duals[None, :], axis=1)
        row_duals = TAU * (loga - lse)
        mass = jnp.exp(row_duals[:, None] + scores)
        column_mass = lax.optimization_barrier(jnp.sum(mass, axis=0))
        duals = TAU * (jnp.log(cluster_mass) - jnp.log(column_mass))
    plan = mass.astype(jnp.bfloat16)
    numerator = lax.dot_general(plan, documents, (((0,), (0,)), ((), ())), preferred_element_type=jnp.float32)
    new_centroids = (numerator / column_mass[:, None]).astype(jnp.bfloat16)
    return (new_centroids, duals)
```

```python
import functools
import math

import jax
import jax.numpy as jnp
from jax import lax
from jax.experimental import pallas as pl
from jax.experimental.pallas import tpu as pltpu
from jax.sharding import PartitionSpec as P

ITERS = 3
TAU = 0.8
TEMP = 4.0
LANES = 128
TILE = 256
F32, BF16 = jnp.float32, jnp.bfloat16
MESH = pl.DeviceIdType.MESH


def kernel(n_rows, n_sub, docs_hbm, cent_hbm, cmass_ref, out_hbm, duals_ref,
           docs, cent, scores, plan, dual_b, acc, col, p1, p2, core_s, core_r, own, y_s, y_r, r_s, r_r, gath,
           in_sem, out_sem, p1_ss, p1_rs, p2_ss, p2_rs, c_ss, c_rs, y_ss, y_rs, r_ss, r_rs, gz_ss, gz_rs, gx_ss, gx_rs):
    n_docs, d = docs.shape
    k_all = cent.shape[0]
    slab = k_all // n_sub
    rps = slab // LANES
    h, w = own.shape[1:]
    nbh = slab // h
    n_ct = d // TILE
    bpc = n_rows // n_ct
    r, s = lax.axis_index("rows"), lax.axis_index("sub")
    s1 = s + 1 - 2 * lax.rem(s, 2)
    s2 = lax.rem(s + 2, n_sub)
    s3 = n_sub - 1 - s
    order = (s3, s1, s2, s)
    r1 = r + 1 - 2 * lax.rem(r, 2)

    barrier = pltpu.get_barrier_semaphore()
    for t in (s1, s2, s3):
        pl.semaphore_signal(barrier, inc=1, device_id=(r, t), device_id_type=MESH)

    def greet(i, _):
        pl.semaphore_signal(barrier, inc=1, device_id=(lax.rem(r + i, n_rows), s), device_id_type=MESH)
        return 0

    lax.fori_loop(1, n_rows, greet, 0)

    def cent_copy(l):
        rows = pl.ds(pl.multiple_of(order[l] * slab, slab), slab)
        return pltpu.make_async_copy(cent_hbm.at[rows, :], cent.at[pl.ds(l * slab, slab), :], in_sem.at[l])

    def docs_copy(c):
        rows = pl.ds(pl.multiple_of(c * TILE, TILE), TILE)
        return pltpu.make_async_copy(docs_hbm.at[rows, :], docs.at[rows, :], in_sem.at[n_sub + c])

    n_chunks = n_docs // TILE
    docs_copy(0).start()
    for l in range(n_sub):
        cent_copy(l).start()
    for c in range(1, n_chunks):
        docs_copy(c).start()
    for l in range(n_sub):
        cent_copy(l).wait()

    scale = TEMP / math.sqrt(d)
    loga = -math.log(n_docs * n_rows * n_sub)

    def fold(read, op, axis_op):
        size = k_all // 8
        parts = [axis_op(read(pl.ds(q * size, size)).reshape(size // 8, 8, LANES), axis=0) for q in range(8)]
        while len(parts) > 1:
            parts = [op(a, b) for a, b in zip(parts[::2], parts[1::2])]
        return axis_op(parts[0], axis=0, keepdims=True)

    def chunk(it, c):
        for u in range(TILE // LANES):
            cols = pl.ds(pl.multiple_of(c * TILE + u * LANES, LANES), LANES)
            if it == 0:
                read = lambda ks: scores[ks, cols]
            else:
                read = lambda ks: scores[ks, cols] + dual_b[ks, :]
            top = fold(read, jnp.maximum, jnp.max)
            total = fold(lambda ks: jnp.exp(read(ks) - top), jnp.add, jnp.sum)
            row_dual = TAU * (loga - (top + jnp.log(total)))
            mass = jnp.exp(scores[:, cols] + row_dual)
            acc[...] += mass
            if it == ITERS - 1:
                plan[:, cols] = mass.astype(BF16)

    def first(c, _):
        docs_copy(c).wait()
        rows = pl.ds(pl.multiple_of(c * TILE, TILE), TILE)
        scores[:, rows] = lax.dot_general(
            cent[...], docs[rows, :], (((1,), (1,)), ((), ())), preferred_element_type=F32
        ) * scale
        chunk(0, c)
        return 0

    def later(it, c, _):
        chunk(it, c)
        return 0

    def p1_copy(it, i):
        t = (s1, s2, s3)[i]
        return pltpu.make_async_remote_copy(
            p1.at[it, s], p1.at[it, s], p1_ss.at[it, i], p1_rs.at[it, i], device_id=(r, t), device_id_type=MESH
        )

    def p1_arrival(it, i):
        t = (s1, s2, s3)[i]
        return pltpu.make_async_remote_copy(
            p1.at[it, t], p1.at[it, t], p1_ss.at[it, i], p1_rs.at[it, i], device_id=(r, t), device_id_type=MESH
        )

    def p2_copy(it, i):
        t = lax.rem(r + i, n_rows)
        return pltpu.make_async_remote_copy(
            p2.at[it, r], p2.at[it, r], p2_ss.at[it, i], p2_rs.at[it, i], device_id=(t, s), device_id_type=MESH
        )

    def p2_arrival(it, i):
        t = lax.rem(r - i + n_rows, n_rows)
        return pltpu.make_async_remote_copy(
            p2.at[it, t], p2.at[it, t], p2_ss.at[it, i], p2_rs.at[it, i], device_id=(t, s), device_id_type=MESH
        )

    def over(start, n, f):
        def body(i, _):
            f(i)
            return 0
        lax.fori_loop(start, n, body, 0)

    def mass_send(it):
        for l in range(n_sub):
            for j in range(rps):
                block = acc[pl.ds(l * slab + j * LANES, LANES), :]
                p1[it, s, pl.ds(order[l] * rps + j, 1), :] = jnp.sum(block.T, axis=0, keepdims=True)
        for i in range(3):
            p1_copy(it, i).start()

    def mass_mid(it):
        for i in range(3):
            p1_arrival(it, i).wait_recv()
        p2[it, r] = (p1[it, 0] + p1[it, 1]) + (p1[it, 2] + p1[it, 3])
        over(1, n_rows, lambda i: p2_copy(it, i).start())

    def spread(value_ref, first_slab):
        for l in range(first_slab, n_sub):
            for j in range(rps):
                row = value_ref[pl.ds(order[l] * rps + j, 1), :]
                dual_b[pl.ds(l * slab + j * LANES, LANES), :] = jnp.broadcast_to(row, (LANES, LANES)).T

    def mass_end(it):
        over(1, n_rows, lambda i: p2_arrival(it, i).wait_recv())
        col[...] = lax.fori_loop(1, n_rows, lambda i, a: a + p2[it, i], p2[it, 0])
        duals_ref[...] = TAU * (jnp.log(cmass_ref[...]) - jnp.log(col[...]))
        if it < ITERS - 1:
            spread(duals_ref, 0)
        else:
            spread(col, n_sub - 1)
        for i in range(3):
            p1_copy(it, i).wait_send()
        over(1, n_rows, lambda i: p2_copy(it, i).wait_send())

    for it in range(ITERS):
        acc[...] = jnp.zeros_like(acc)
        lax.fori_loop(0, n_chunks, first if it == 0 else functools.partial(later, it), 0)
        if it == 0:
            pl.semaphore_wait(barrier, 3 + n_rows - 1)
        mass_send(it)
        if it < ITERS - 1:
            mass_mid(it)
            mass_end(it)

    tiles = [lax.rem(lax.div(r, bpc) + 1 + j, n_ct) for j in range(n_ct)]

    def product(first_row, j):
        cols = pl.ds(pl.multiple_of(tiles[j] * TILE, TILE), TILE)
        return jnp.dot(plan[pl.ds(first_row, 2 * slab), :], docs[:, cols], preferred_element_type=F32)

    def core_copy(j):
        return pltpu.make_async_remote_copy(
            core_s.at[j], core_r.at[j], c_ss.at[j], c_rs.at[j], device_id=(r, s1), device_id_type=MESH
        )

    def y_copy(m):
        return pltpu.make_async_remote_copy(
            y_s.at[m], y_r.at[m], y_ss.at[m], y_rs.at[m], device_id=(r, s2), device_id_type=MESH
        )

    def far(j):
        core_s[j] = product(0, j)
        core_copy(j).start()

    def near(j):
        both = product(2 * slab, j)
        core_copy(j).wait_recv()
        both = both + core_r[j]
        for q in range(bpc):
            m, i, c = j * bpc + q, (q % nbh) * h, (q // nbh) * w
            y_s[m] = both[i:i + h, c:c + w].astype(BF16)
            y_copy(m).start()
            own[m] = both[slab + i:slab + i + h, c:c + w]

    far(0)
    far(1)
    mass_mid(ITERS - 1)
    near(0)
    for j in range(1, n_ct):
        if j + 1 < n_ct:
            far(j + 1)
        near(j)

    def block_of(m):
        return tiles[m // bpc] * bpc + m % bpc

    def r_copy(m):
        b = block_of(m)
        return pltpu.make_async_remote_copy(
            r_s.at[m], r_r.at[r], r_ss.at[m], r_rs.at[r], device_id=(b, s), device_id_type=MESH
        )

    def r_arrival(t):
        return pltpu.make_async_remote_copy(
            r_r.at[t], r_r.at[t], r_ss.at[0], r_rs.at[t], device_id=(t, s), device_id_type=MESH
        )

    for m in range(n_rows):
        y_copy(m).wait_recv()
        value = own[m] + y_r[m].astype(F32)
        if m < n_rows - bpc:
            r_s[m] = value.astype(BF16)
            r_copy(m).start()
        else:
            own[m] = value

            @pl.when(block_of(m) != r)
            def _():
                r_s[m] = own[m].astype(BF16)
                r_copy(m).start()

    mass_end(ITERS - 1)

    mine = own[n_rows - bpc + lax.rem(r, bpc)]

    def gather_sum(i, total):
        t = lax.rem(r - i + n_rows, n_rows)
        r_arrival(t).wait_recv()
        return total + r_r[t].astype(F32)

    total = lax.fori_loop(1, n_rows, gather_sum, mine)
    i0 = pl.multiple_of((n_sub - 1) * slab + lax.rem(r, nbh) * h, h)
    gath[r] = (total / dual_b[pl.ds(i0, h), :]).astype(BF16)

    half = n_rows // 2

    def z_copy(i):
        return pltpu.make_async_remote_copy(
            gath.at[r], gath.at[r], gz_ss.at[i], gz_rs.at[i],
            device_id=(lax.rem(r + 2 * i, n_rows), s), device_id_type=MESH,
        )

    def z_arrival(i):
        t = lax.rem(r - 2 * i + n_rows, n_rows)
        return pltpu.make_async_remote_copy(
            gath.at[t], gath.at[t], gz_ss.at[i], gz_rs.at[i], device_id=(t, s), device_id_type=MESH
        )

    def x_copy(i):
        t = lax.rem(r - 2 * i + n_rows, n_rows)
        return pltpu.make_async_remote_copy(
            gath.at[t], gath.at[t], gx_ss.at[i], gx_rs.at[i], device_id=(r1, s), device_id_type=MESH
        )

    def x_arrival(i):
        t = lax.rem(r1 - 2 * i + n_rows, n_rows)
        return pltpu.make_async_remote_copy(
            gath.at[t], gath.at[t], gx_ss.at[i], gx_rs.at[i], device_id=(r1, s), device_id_type=MESH
        )

    def store(b, i):
        rows = pl.ds(pl.multiple_of(lax.rem(b, nbh) * h, h), h)
        cols = pl.ds(pl.multiple_of(lax.div(b, nbh) * w, w), w)
        return pltpu.make_async_copy(gath.at[b], out_hbm.at[rows, cols], out_sem.at[i])

    over(1, half, lambda i: z_copy(i).start())
    x_copy(0).start()
    store(r, 0).start()

    def forward(i):
        z_arrival(i).wait_recv()
        x_copy(i).start()
        store(lax.rem(r - 2 * i + n_rows, n_rows), i).start()

    over(1, half, forward)

    def keep(i):
        x_arrival(i).wait_recv()
        store(lax.rem(r1 - 2 * i + n_rows, n_rows), half + i).start()

    over(0, half, keep)

    for j in range(n_ct):
        core_copy(j).wait_send()
    over(0, n_rows, lambda m: y_copy(m).wait_send())
    for m in range(n_rows):
        if m < n_rows - bpc:
            r_copy(m).wait_send()
        else:
            @pl.when(block_of(m) != r)
            def _():
                r_copy(m).wait_send()
    over(1, half, lambda i: z_copy(i).wait_send())
    over(0, half, lambda i: x_copy(i).wait_send())
    over(0, half, lambda i: store(lax.rem(r - 2 * i + n_rows, n_rows), i).wait())
    over(0, half, lambda i: store(lax.rem(r1 - 2 * i + n_rows, n_rows), half + i).wait())


def per_device(n_rows, n_sub, documents, centroids, cluster_mass):
    n_docs, d = documents.shape
    k = centroids.shape[0]
    slab = k // n_sub
    n_ct = d // TILE
    w = LANES
    h = slab * d // (w * n_rows)
    dma = pltpu.SemaphoreType.DMA
    vm = pltpu.VMEM
    blocks = (n_rows, h, w)
    out, duals = pl.pallas_call(
        functools.partial(kernel, n_rows, n_sub),
        out_shape=(
            jax.ShapeDtypeStruct((slab, d), BF16),
            jax.ShapeDtypeStruct((k // LANES, LANES), F32),
        ),
        in_specs=[
            pl.BlockSpec(memory_space=pl.ANY),
            pl.BlockSpec(memory_space=pl.ANY),
            pl.BlockSpec(memory_space=pltpu.VMEM),
        ],
        out_specs=(pl.BlockSpec(memory_space=pl.ANY), pl.BlockSpec(memory_space=pltpu.VMEM)),
        scratch_shapes=[
            vm((n_docs, d), BF16), vm((k, d), BF16), vm((k, n_docs), F32), vm((k, n_docs), BF16),
            vm((k, LANES), F32), vm((k, LANES), F32), vm((k // LANES, LANES), F32),
            vm((ITERS, n_sub, k // LANES, LANES), F32), vm((ITERS, n_rows, k // LANES, LANES), F32),
            vm((n_ct, 2 * slab, TILE), F32), vm((n_ct, 2 * slab, TILE), F32),
            vm(blocks, F32), vm(blocks, BF16), vm(blocks, BF16), vm(blocks, BF16), vm(blocks, BF16), vm(blocks, BF16),
            dma((n_sub + n_docs // TILE,)), dma((n_rows,)),
            dma((ITERS, 3)), dma((ITERS, 3)), dma((ITERS, n_rows)), dma((ITERS, n_rows)),
            dma((n_ct,)), dma((n_ct,)), dma((n_rows,)), dma((n_rows,)), dma((n_rows,)), dma((n_rows,)),
            dma((n_rows // 2,)), dma((n_rows // 2,)), dma((n_rows // 2,)), dma((n_rows // 2,)),
        ],
        compiler_params=pltpu.CompilerParams(
            collective_id=0, has_side_effects=True, vmem_limit_bytes=48 * 1024 * 1024
        ),
        cost_estimate=pl.CostEstimate(
            flops=4 * n_docs * k * d, bytes_accessed=2 * (n_docs * d + k * d + slab * d),
            transcendentals=2 * ITERS * n_docs * k,
        ),
    )(documents, centroids, cluster_mass.reshape(k // LANES, LANES))
    return out, duals.reshape(k)


def solution(mesh):
    return jax.shard_map(
        functools.partial(per_device, mesh.shape["rows"], mesh.shape["sub"]),
        mesh=mesh,
        in_specs=(P(("rows", "sub"), None), P(), P()),
        out_specs=(P("sub", None), P()),
        check_vma=False,
    )
```

```python
import functools
import math

import jax
import jax.numpy as jnp
from jax import lax
from jax.experimental import pallas as pl
from jax.experimental.pallas import tpu as pltpu
from jax.sharding import PartitionSpec as P

ITERS = 3
TAU = 0.8
TEMP = 4.0
LOG2E = math.log2(math.e)
HEADROOM = 112.0
LANES = 128
TILE = 256
F32, BF16 = jnp.float32, jnp.bfloat16
MESH = pl.DeviceIdType.MESH


def kernel(n_rows, n_sub, docs_hbm, cent_hbm, cmass_hbm, out_hbm, duals_ref,
           docs, cent, scores, plan, dual_b, acc, col, cmass, shifted, adjust, lse, p1, p2, core_s, core_r, own, y_s, y_r, r_s, r_r, gath,
           in_sem, out_sem, p1_ss, p1_rs, p2_ss, p2_rs, c_ss, c_rs, y_ss, y_rs, r_ss, r_rs, gz_ss, gz_rs, gx_ss, gx_rs):
    n_docs, d = docs.shape
    k_all = cent.shape[0]
    slab = k_all // n_sub
    rps = slab // LANES
    h, w = own.shape[1:]
    nbh = slab // h
    n_ct = d // TILE
    bpc = n_rows // n_ct
    r, s = lax.axis_index("rows"), lax.axis_index("sub")
    s1 = s + 1 - 2 * lax.rem(s, 2)
    s2 = lax.rem(s + 2, n_sub)
    s3 = n_sub - 1 - s
    order = (s3, s1, s2, s)
    r1 = r + 1 - 2 * lax.rem(r, 2)

    barrier = pltpu.get_barrier_semaphore()
    for t in (s1, s2, s3):
        pl.semaphore_signal(barrier, inc=1, device_id=(r, t), device_id_type=MESH)

    def greet(i, _):
        pl.semaphore_signal(barrier, inc=1, device_id=(lax.rem(r + i, n_rows), s), device_id_type=MESH)
        return 0

    lax.fori_loop(1, n_rows, greet, 0)

    def cent_copy(l):
        rows = pl.ds(pl.multiple_of(order[l] * slab, slab), slab)
        return pltpu.make_async_copy(cent_hbm.at[rows, :], cent.at[pl.ds(l * slab, slab), :], in_sem.at[l])

    def docs_copy(c):
        rows = pl.ds(pl.multiple_of(c * TILE, TILE), TILE)
        return pltpu.make_async_copy(docs_hbm.at[rows, :], docs.at[rows, :], in_sem.at[n_sub + c])

    n_chunks = n_docs // TILE
    docs_copy(0).start()
    for l in range(n_sub):
        cent_copy(l).start()
    for c in range(1, n_chunks):
        docs_copy(c).start()
    cmass_copy = pltpu.make_async_copy(cmass_hbm, cmass, in_sem.at[n_sub + n_chunks])
    cmass_copy.start()
    for l in range(n_sub):
        cent_copy(l).wait()
    cmass_copy.wait()

    scale = TEMP / math.sqrt(d) * LOG2E
    loga = -math.log2(n_docs * n_rows * n_sub)
    parts = 8
    size = k_all // parts
    slices = [pl.ds(q * size, size) for q in range(parts)]

    def halves(c):
        return [pl.ds(pl.multiple_of(c * TILE + u * LANES, LANES), LANES) for u in range(TILE // LANES)]

    def eight(value, axis_op):
        return axis_op(value.reshape(size // 8, 8, LANES), axis=0)

    def tree(values, op, axis_op):
        while len(values) > 1:
            values = [op(a, b) for a, b in zip(values[::2], values[1::2])]
        return axis_op(values[0], axis=0, keepdims=True)

    def mass_slice(it, ks, cols, row_duals):
        masses = [jnp.exp2(scores[ks, cu] + rd) for cu, rd in zip(cols, row_duals)]
        acc[ks, :] += sum(masses[1:], masses[0])
        if it == ITERS - 1:
            for cu, mass in zip(cols, masses):
                plan[ks, cu] = mass.astype(BF16)

    def step(it, following, current, row_duals):
        sums = None
        if following is not None:
            cols = halves(following)
            if it == 0:
                shift = [
                    tree([eight(scores[ks, cu], jnp.max) for ks in slices], jnp.maximum, jnp.max) for cu in cols
                ]
            else:
                shift = [lse[:, cu] for cu in cols]
            sums = [[] for _ in cols]
        for ks in slices:
            if following is not None:
                for cu, top, out in zip(cols, shift, sums):
                    x = scores[ks, cu] if it == 0 else scores[ks, cu] + dual_b[ks, :]
                    out.append(eight(jnp.exp2(x - top), jnp.sum))
            if current is not None:
                mass_slice(it, ks, halves(current), row_duals)
        if following is None:
            return None
        result = []
        for cu, top, values in zip(cols, shift, sums):
            value = top + jnp.log(tree(values, jnp.add, jnp.sum)) * LOG2E
            if it > 0:
                value = value + adjust[...]
            lse[:, cu] = value
            result.append(TAU * (loga - value))
        return tuple(result)

    def first_pass():
        row_duals = None
        for c in range(n_chunks + 2):
            if c < n_chunks:
                docs_copy(c).wait()
                rows = pl.ds(c * TILE, TILE)
                scores[:, rows] = lax.dot_general(
                    cent[...], docs[rows, :], (((1,), (1,)), ((), ())), preferred_element_type=F32
                ) * scale
            if c >= 1:
                row_duals = step(0, c - 1 if c <= n_chunks else None, c - 2 if c >= 2 else None, row_duals)

    def later_pass(it):
        row_duals = step(it, 0, None, None)
        row_duals = lax.fori_loop(0, n_chunks - 1, lambda c, rd: step(it, c + 1, c, rd), row_duals)
        step(it, None, n_chunks - 1, row_duals)

    def p1_copy(it, i):
        t = (s1, s2, s3)[i]
        return pltpu.make_async_remote_copy(
            p1.at[it, s], p1.at[it, s], p1_ss.at[it, i], p1_rs.at[it, i], device_id=(r, t), device_id_type=MESH
        )

    def p1_arrival(it, i):
        t = (s1, s2, s3)[i]
        return pltpu.make_async_remote_copy(
            p1.at[it, t], p1.at[it, t], p1_ss.at[it, i], p1_rs.at[it, i], device_id=(r, t), device_id_type=MESH
        )

    def p2_copy(it, i):
        t = lax.rem(r + i, n_rows)
        return pltpu.make_async_remote_copy(
            p2.at[it, r], p2.at[it, r], p2_ss.at[it, i], p2_rs.at[it, i], device_id=(t, s), device_id_type=MESH
        )

    def p2_arrival(it, i):
        t = lax.rem(r - i + n_rows, n_rows)
        return pltpu.make_async_remote_copy(
            p2.at[it, t], p2.at[it, t], p2_ss.at[it, i], p2_rs.at[it, i], device_id=(t, s), device_id_type=MESH
        )

    def over(start, n, f):
        def body(i, _):
            f(i)
            return 0
        lax.fori_loop(start, n, body, 0)

    def mass_send(it):
        for l in range(n_sub):
            for j in range(rps):
                block = acc[pl.ds(l * slab + j * LANES, LANES), :]
                p1[it, s, pl.ds(order[l] * rps + j, 1), :] = jnp.sum(block.T, axis=0, keepdims=True)
        for i in range(3):
            p1_copy(it, i).start()

    def mass_mid(it):
        for i in range(3):
            p1_arrival(it, i).wait_recv()
        p2[it, r] = (p1[it, 0] + p1[it, 1]) + (p1[it, 2] + p1[it, 3])
        over(1, n_rows, lambda i: p2_copy(it, i).start())

    def spread(value_ref, first_slab):
        for l in range(first_slab, n_sub):
            for j in range(rps):
                row = value_ref[pl.ds(order[l] * rps + j, 1), :]
                dual_b[pl.ds(l * slab + j * LANES, LANES), :] = jnp.broadcast_to(row, (LANES, LANES)).T

    def mass_end(it):
        over(1, n_rows, lambda i: p2_arrival(it, i).wait_recv())
        col[...] = lax.fori_loop(1, n_rows, lambda i, a: a + p2[it, i], p2[it, 0])
        new = TAU * (jnp.log(cmass[...]) - jnp.log(col[...]))
        if it < ITERS - 1:
            change = LOG2E * (new if it == 0 else new - duals_ref[...])
            most = jnp.max(jnp.max(change, axis=0, keepdims=True), axis=1, keepdims=True)
            adjust[...] = jnp.broadcast_to(most - HEADROOM, adjust.shape)
            shifted[...] = LOG2E * new - (most - HEADROOM)
            duals_ref[...] = new
            spread(shifted, 0)
        else:
            duals_ref[...] = new
            spread(col, n_sub - 1)
        for i in range(3):
            p1_copy(it, i).wait_send()
        over(1, n_rows, lambda i: p2_copy(it, i).wait_send())

    for it in range(ITERS):
        acc[...] = jnp.zeros_like(acc)
        if it == 0:
            first_pass()
        else:
            later_pass(it)
        if it == 0:
            pl.semaphore_wait(barrier, 3 + n_rows - 1)
        mass_send(it)
        if it < ITERS - 1:
            mass_mid(it)
            mass_end(it)

    tiles = [lax.rem(lax.div(r, bpc) + 1 + j, n_ct) for j in range(n_ct)]

    def product(first_row, j):
        cols = pl.ds(pl.multiple_of(tiles[j] * TILE, TILE), TILE)
        return jnp.dot(plan[pl.ds(first_row, 2 * slab), :], docs[:, cols], preferred_element_type=F32)

    def core_copy(j):
        return pltpu.make_async_remote_copy(
            core_s.at[j], core_r.at[j], c_ss.at[j], c_rs.at[j], device_id=(r, s1), device_id_type=MESH
        )

    def y_copy(m):
        return pltpu.make_async_remote_copy(
            y_s.at[m], y_r.at[m], y_ss.at[m], y_rs.at[m], device_id=(r, s2), device_id_type=MESH
        )

    def far(j):
        core_s[j] = product(0, j)
        core_copy(j).start()

    def near(j):
        both = product(2 * slab, j)
        core_copy(j).wait_recv()
        both = both + core_r[j]
        for q in range(bpc):
            m, i, c = j * bpc + q, (q % nbh) * h, (q // nbh) * w
            y_s[m] = both[i:i + h, c:c + w].astype(BF16)
            y_copy(m).start()
            own[m] = both[slab + i:slab + i + h, c:c + w]

    far(0)
    far(1)
    mass_mid(ITERS - 1)
    near(0)
    for j in range(1, n_ct):
        if j + 1 < n_ct:
            far(j + 1)
        near(j)

    def block_of(m):
        return tiles[m // bpc] * bpc + m % bpc

    def r_copy(m):
        b = block_of(m)
        return pltpu.make_async_remote_copy(
            r_s.at[m], r_r.at[r], r_ss.at[m], r_rs.at[r], device_id=(b, s), device_id_type=MESH
        )

    def r_arrival(t):
        return pltpu.make_async_remote_copy(
            r_r.at[t], r_r.at[t], r_ss.at[0], r_rs.at[t], device_id=(t, s), device_id_type=MESH
        )

    for m in range(n_rows):
        y_copy(m).wait_recv()
        value = own[m] + y_r[m].astype(F32)
        if m < n_rows - bpc:
            r_s[m] = value.astype(BF16)
            r_copy(m).start()
        else:
            own[m] = value

            @pl.when(block_of(m) != r)
            def _():
                r_s[m] = own[m].astype(BF16)
                r_copy(m).start()

    mass_end(ITERS - 1)

    mine = own[n_rows - bpc + lax.rem(r, bpc)]

    def gather_sum(i, total):
        t = lax.rem(r - i + n_rows, n_rows)
        r_arrival(t).wait_recv()
        return total + r_r[t].astype(F32)

    total = lax.fori_loop(1, n_rows, gather_sum, mine)
    i0 = pl.multiple_of((n_sub - 1) * slab + lax.rem(r, nbh) * h, h)
    gath[r] = (total / dual_b[pl.ds(i0, h), :]).astype(BF16)

    half = n_rows // 2

    def z_copy(i):
        return pltpu.make_async_remote_copy(
            gath.at[r], gath.at[r], gz_ss.at[i], gz_rs.at[i],
            device_id=(lax.rem(r + 2 * i, n_rows), s), device_id_type=MESH,
        )

    def z_arrival(i):
        t = lax.rem(r - 2 * i + n_rows, n_rows)
        return pltpu.make_async_remote_copy(
            gath.at[t], gath.at[t], gz_ss.at[i], gz_rs.at[i], device_id=(t, s), device_id_type=MESH
        )

    def x_copy(i):
        t = lax.rem(r - 2 * i + n_rows, n_rows)
        return pltpu.make_async_remote_copy(
            gath.at[t], gath.at[t], gx_ss.at[i], gx_rs.at[i], device_id=(r1, s), device_id_type=MESH
        )

    def x_arrival(i):
        t = lax.rem(r1 - 2 * i + n_rows, n_rows)
        return pltpu.make_async_remote_copy(
            gath.at[t], gath.at[t], gx_ss.at[i], gx_rs.at[i], device_id=(r1, s), device_id_type=MESH
        )

    def store(b, i):
        rows = pl.ds(pl.multiple_of(lax.rem(b, nbh) * h, h), h)
        cols = pl.ds(pl.multiple_of(lax.div(b, nbh) * w, w), w)
        return pltpu.make_async_copy(gath.at[b], out_hbm.at[rows, cols], out_sem.at[i])

    over(1, half, lambda i: z_copy(i).start())
    x_copy(0).start()
    store(r, 0).start()

    def forward(i):
        z_arrival(i).wait_recv()
        x_copy(i).start()
        store(lax.rem(r - 2 * i + n_rows, n_rows), i).start()

    over(1, half, forward)

    def keep(i):
        x_arrival(i).wait_recv()
        store(lax.rem(r1 - 2 * i + n_rows, n_rows), half + i).start()

    over(0, half, keep)

    for j in range(n_ct):
        core_copy(j).wait_send()
    over(0, n_rows, lambda m: y_copy(m).wait_send())
    for m in range(n_rows):
        if m < n_rows - bpc:
            r_copy(m).wait_send()
        else:
            @pl.when(block_of(m) != r)
            def _():
                r_copy(m).wait_send()
    over(1, half, lambda i: z_copy(i).wait_send())
    over(0, half, lambda i: x_copy(i).wait_send())
    over(0, half, lambda i: store(lax.rem(r - 2 * i + n_rows, n_rows), i).wait())
    over(0, half, lambda i: store(lax.rem(r1 - 2 * i + n_rows, n_rows), half + i).wait())


def per_device(n_rows, n_sub, documents, centroids, cluster_mass):
    n_docs, d = documents.shape
    k = centroids.shape[0]
    slab = k // n_sub
    n_ct = d // TILE
    w = LANES
    h = slab * d // (w * n_rows)
    dma = pltpu.SemaphoreType.DMA
    vm = pltpu.VMEM
    blocks = (n_rows, h, w)
    out, duals = pl.pallas_call(
        functools.partial(kernel, n_rows, n_sub),
        out_shape=(
            jax.ShapeDtypeStruct((slab, d), BF16),
            jax.ShapeDtypeStruct((k // LANES, LANES), F32),
        ),
        in_specs=[
            pl.BlockSpec(memory_space=pl.ANY),
            pl.BlockSpec(memory_space=pl.ANY),
            pl.BlockSpec(memory_space=pl.ANY),
        ],
        out_specs=(pl.BlockSpec(memory_space=pl.ANY), pl.BlockSpec(memory_space=pltpu.VMEM)),
        scratch_shapes=[
            vm((n_docs, d), BF16), vm((k, d), BF16), vm((k, n_docs), F32), vm((k, n_docs), BF16),
            vm((k, LANES), F32), vm((k, LANES), F32),
            vm((k // LANES, LANES), F32), vm((k // LANES, LANES), F32), vm((k // LANES, LANES), F32), vm((1, LANES), F32), vm((1, n_docs), F32),
            vm((ITERS, n_sub, k // LANES, LANES), F32), vm((ITERS, n_rows, k // LANES, LANES), F32),
            vm((n_ct, 2 * slab, TILE), F32), vm((n_ct, 2 * slab, TILE), F32),
            vm(blocks, F32), vm(blocks, BF16), vm(blocks, BF16), vm(blocks, BF16), vm(blocks, BF16), vm(blocks, BF16),
            dma((n_sub + n_docs // TILE + 1,)), dma((n_rows,)),
            dma((ITERS, 3)), dma((ITERS, 3)), dma((ITERS, n_rows)), dma((ITERS, n_rows)),
            dma((n_ct,)), dma((n_ct,)), dma((n_rows,)), dma((n_rows,)), dma((n_rows,)), dma((n_rows,)),
            dma((n_rows // 2,)), dma((n_rows // 2,)), dma((n_rows // 2,)), dma((n_rows // 2,)),
        ],
        compiler_params=pltpu.CompilerParams(
            collective_id=0, has_side_effects=True, vmem_limit_bytes=60 * 1024 * 1024
        ),
        cost_estimate=pl.CostEstimate(
            flops=4 * n_docs * k * d, bytes_accessed=2 * (n_docs * d + k * d + slab * d),
            transcendentals=2 * ITERS * n_docs * k,
        ),
    )(documents, centroids, cluster_mass.reshape(k // LANES, LANES))
    return out, duals.reshape(k)


def solution(mesh):
    return jax.shard_map(
        functools.partial(per_device, mesh.shape["rows"], mesh.shape["sub"]),
        mesh=mesh,
        in_specs=(P(("rows", "sub"), None), P(), P()),
        out_specs=(P("sub", None), P()),
        check_vma=False,
    )
```

```python
import functools
import math

import jax
import jax.numpy as jnp
from jax import lax
from jax.experimental import pallas as pl
from jax.experimental.pallas import tpu as pltpu
from jax.sharding import PartitionSpec as P

ITERS = 3
TAU = 0.8
TEMP = 4.0
LOG2E = math.log2(math.e)
HEADROOM = 112.0
LANES = 128
TILE = 256
F32, BF16 = jnp.float32, jnp.bfloat16
MESH = pl.DeviceIdType.MESH


def kernel(n_rows, n_sub, docs_hbm, cent_hbm, cmass_hbm, out_hbm, duals_ref,
           docs, cent, scores, plan, dual_b, acc, col, cmass, shifted, adjust, lse, p1, p2, core_s, core_r, own, y_s, y_r, r_s, r_r, gath,
           in_sem, out_sem, p1_ss, p1_rs, p2_ss, p2_rs, c_ss, c_rs, y_ss, y_rs, r_ss, r_rs, gz_ss, gz_rs, gx_ss, gx_rs):
    n_docs, d = docs.shape
    k_all = cent.shape[0]
    slab = k_all // n_sub
    rps = slab // LANES
    h, w = own.shape[1:]
    nbh = slab // h
    n_ct = d // TILE
    bpc = n_rows // n_ct
    r, s = lax.axis_index("rows"), lax.axis_index("sub")
    s1 = s + 1 - 2 * lax.rem(s, 2)
    s2 = lax.rem(s + 2, n_sub)
    s3 = n_sub - 1 - s
    order = (s3, s1, s2, s)
    r1 = r + 1 - 2 * lax.rem(r, 2)

    barrier = pltpu.get_barrier_semaphore()
    for t in (s1, s2, s3):
        pl.semaphore_signal(barrier, inc=1, device_id=(r, t), device_id_type=MESH)

    def greet(i, _):
        pl.semaphore_signal(barrier, inc=1, device_id=(lax.rem(r + i, n_rows), s), device_id_type=MESH)
        return 0

    lax.fori_loop(1, n_rows, greet, 0)

    def cent_copy(l):
        rows = pl.ds(pl.multiple_of(order[l] * slab, slab), slab)
        return pltpu.make_async_copy(cent_hbm.at[rows, :], cent.at[pl.ds(l * slab, slab), :], in_sem.at[l])

    def docs_copy(c):
        rows = pl.ds(pl.multiple_of(c * TILE, TILE), TILE)
        return pltpu.make_async_copy(docs_hbm.at[rows, :], docs.at[rows, :], in_sem.at[n_sub + c])

    n_chunks = n_docs // TILE
    docs_copy(0).start()
    for l in range(n_sub):
        cent_copy(l).start()
    for c in range(1, n_chunks):
        docs_copy(c).start()
    cmass_copy = pltpu.make_async_copy(cmass_hbm, cmass, in_sem.at[n_sub + n_chunks])
    cmass_copy.start()
    for l in range(n_sub):
        cent_copy(l).wait()
    cmass_copy.wait()

    scale = TEMP / math.sqrt(d) * LOG2E
    loga = -math.log2(n_docs * n_rows * n_sub)
    parts = 8
    size = k_all // parts
    slices = [pl.ds(q * size, size) for q in range(parts)]

    def halves(c):
        return [pl.ds(pl.multiple_of(c * TILE + u * LANES, LANES), LANES) for u in range(TILE // LANES)]

    def eight(value, axis_op):
        return axis_op(value.reshape(size // 8, 8, LANES), axis=0)

    def tree(values, op, axis_op):
        while len(values) > 1:
            values = [op(a, b) for a, b in zip(values[::2], values[1::2])]
        return axis_op(values[0], axis=0, keepdims=True)

    def mass_slice(keep, ks, cols, row_duals):
        masses = [jnp.exp2(scores[ks, cu] + rd) for cu, rd in zip(cols, row_duals)]
        acc[ks, :] += sum(masses[1:], masses[0])
        if keep:
            for cu, mass in zip(cols, masses):
                plan[ks, cu] = mass.astype(BF16)

    def step(initial, following, current, row_duals):
        sums = None
        if following is not None:
            cols = halves(following)
            if initial:
                shift = [
                    tree([eight(scores[ks, cu], jnp.max) for ks in slices], jnp.maximum, jnp.max) for cu in cols
                ]
            else:
                shift = [lse[:, cu] for cu in cols]
            sums = [[] for _ in cols]
        for ks in slices:
            if following is not None:
                for cu, top, out in zip(cols, shift, sums):
                    x = scores[ks, cu] if initial else scores[ks, cu] + dual_b[ks, :]
                    out.append(eight(jnp.exp2(x - top), jnp.sum))
            if current is not None:
                mass_slice(True, ks, halves(current), row_duals)
        if following is None:
            return None
        result = []
        for cu, top, values in zip(cols, shift, sums):
            value = top + jnp.log(tree(values, jnp.add, jnp.sum)) * LOG2E
            if not initial:
                value = value + adjust[...]
            lse[:, cu] = value
            result.append(TAU * (loga - value))
        return tuple(result)

    def first_chunk(c):
        docs_copy(c).wait()
        rows = pl.ds(pl.multiple_of(c * TILE, TILE), TILE)
        scores[:, rows] = lax.dot_general(
            cent[...], docs[rows, :], (((1,), (1,)), ((), ())), preferred_element_type=F32
        ) * scale
        row_duals = step(True, c, None, None)
        for ks in slices:
            mass_slice(False, ks, halves(c), row_duals)

    def later_pass():
        row_duals = step(False, 0, None, None)
        row_duals = lax.fori_loop(0, n_chunks - 1, lambda c, rd: step(False, c + 1, c, rd), row_duals)
        step(False, None, n_chunks - 1, row_duals)

    def p1_copy(it, i):
        t = (s1, s2, s3)[i]
        return pltpu.make_async_remote_copy(
            p1.at[it, s], p1.at[it, s], p1_ss.at[it, i], p1_rs.at[it, i], device_id=(r, t), device_id_type=MESH
        )

    def p1_arrival(it, i):
        t = (s1, s2, s3)[i]
        return pltpu.make_async_remote_copy(
            p1.at[it, t], p1.at[it, t], p1_ss.at[it, i], p1_rs.at[it, i], device_id=(r, t), device_id_type=MESH
        )

    def p2_copy(it, i):
        t = lax.rem(r + i, n_rows)
        return pltpu.make_async_remote_copy(
            p2.at[it, r], p2.at[it, r], p2_ss.at[it, i], p2_rs.at[it, i], device_id=(t, s), device_id_type=MESH
        )

    def p2_arrival(it, i):
        t = lax.rem(r - i + n_rows, n_rows)
        return pltpu.make_async_remote_copy(
            p2.at[it, t], p2.at[it, t], p2_ss.at[it, i], p2_rs.at[it, i], device_id=(t, s), device_id_type=MESH
        )

    def over(start, n, f):
        def body(i, _):
            f(i)
            return 0
        lax.fori_loop(start, n, body, 0)

    def mass_send(it):
        for l in range(n_sub):
            for j in range(rps):
                block = acc[pl.ds(l * slab + j * LANES, LANES), :]
                p1[it, s, pl.ds(order[l] * rps + j, 1), :] = jnp.sum(block.T, axis=0, keepdims=True)
        for i in range(3):
            p1_copy(it, i).start()

    def mass_mid(it):
        for i in range(3):
            p1_arrival(it, i).wait_recv()
        p2[it, r] = (p1[it, 0] + p1[it, 1]) + (p1[it, 2] + p1[it, 3])
        over(1, n_rows, lambda i: p2_copy(it, i).start())

    def spread(value_ref, first_slab):
        for l in range(first_slab, n_sub):
            for j in range(rps):
                row = value_ref[pl.ds(order[l] * rps + j, 1), :]
                dual_b[pl.ds(l * slab + j * LANES, LANES), :] = jnp.broadcast_to(row, (LANES, LANES)).T

    def mass_end(it, last):
        over(1, n_rows, lambda i: p2_arrival(it, i).wait_recv())
        col[...] = lax.fori_loop(1, n_rows, lambda i, a: a + p2[it, i], p2[it, 0])
        new = TAU * (jnp.log(cmass[...]) - jnp.log(col[...]))
        if last:
            spread(col, n_sub - 1)
        else:
            change = LOG2E * (new - duals_ref[...])
            most = jnp.max(jnp.max(change, axis=0, keepdims=True), axis=1, keepdims=True)
            adjust[...] = jnp.broadcast_to(most - HEADROOM, adjust.shape)
            shifted[...] = LOG2E * new - (most - HEADROOM)
            spread(shifted, 0)
        duals_ref[...] = new
        for i in range(3):
            p1_copy(it, i).wait_send()
        over(1, n_rows, lambda i: p2_copy(it, i).wait_send())

    acc[...] = jnp.zeros_like(acc)
    duals_ref[...] = jnp.zeros_like(duals_ref)
    over(0, n_chunks, first_chunk)
    pl.semaphore_wait(barrier, 3 + n_rows - 1)
    mass_send(0)

    def iteration(it):
        mass_mid(it - 1)
        mass_end(it - 1, False)
        acc[...] = jnp.zeros_like(acc)
        later_pass()
        mass_send(it)

    over(1, ITERS, iteration)

    def tile_of(j):
        return lax.rem(lax.div(r, bpc) + 1 + j, n_ct)

    def product(first_row, j):
        cols = pl.ds(pl.multiple_of(tile_of(j) * TILE, TILE), TILE)
        return jnp.dot(plan[pl.ds(first_row, 2 * slab), :], docs[:, cols], preferred_element_type=F32)

    def core_copy(j):
        return pltpu.make_async_remote_copy(
            core_s.at[j], core_r.at[j], c_ss.at[j], c_rs.at[j], device_id=(r, s1), device_id_type=MESH
        )

    def y_copy(m):
        return pltpu.make_async_remote_copy(
            y_s.at[m], y_r.at[m], y_ss.at[m], y_rs.at[m], device_id=(r, s2), device_id_type=MESH
        )

    def far(j):
        core_s[j] = product(0, j)
        core_copy(j).start()

    def near(j):
        both = product(2 * slab, j)
        core_copy(j).wait_recv()
        both = both + core_r[j]
        for q in range(bpc):
            m, i, c = j * bpc + q, (q % nbh) * h, (q // nbh) * w
            y_s[m] = both[i:i + h, c:c + w].astype(BF16)
            y_copy(m).start()
            own[m] = both[slab + i:slab + i + h, c:c + w]

    over(0, n_ct, far)
    mass_mid(ITERS - 1)
    over(0, n_ct, near)

    def block_of(m):
        return tile_of(lax.div(m, bpc)) * bpc + lax.rem(m, bpc)

    def r_copy(m):
        b = block_of(m)
        return pltpu.make_async_remote_copy(
            r_s.at[m], r_r.at[r], r_ss.at[m], r_rs.at[r], device_id=(b, s), device_id_type=MESH
        )

    def r_arrival(t):
        return pltpu.make_async_remote_copy(
            r_r.at[t], r_r.at[t], r_ss.at[0], r_rs.at[t], device_id=(t, s), device_id_type=MESH
        )

    def reduce_block(m):
        y_copy(m).wait_recv()
        own[m] = own[m] + y_r[m].astype(F32)

        @pl.when(block_of(m) != r)
        def _():
            r_s[m] = own[m].astype(BF16)
            r_copy(m).start()

    over(0, n_rows, reduce_block)
    mass_end(ITERS - 1, True)

    mine = own[n_rows - bpc + lax.rem(r, bpc)]

    def gather_sum(i, total):
        t = lax.rem(r - i + n_rows, n_rows)
        r_arrival(t).wait_recv()
        return total + r_r[t].astype(F32)

    total = lax.fori_loop(1, n_rows, gather_sum, mine)
    i0 = pl.multiple_of((n_sub - 1) * slab + lax.rem(r, nbh) * h, h)
    gath[r] = (total / dual_b[pl.ds(i0, h), :]).astype(BF16)

    half = n_rows // 2

    def z_copy(i):
        return pltpu.make_async_remote_copy(
            gath.at[r], gath.at[r], gz_ss.at[i], gz_rs.at[i],
            device_id=(lax.rem(r + 2 * i, n_rows), s), device_id_type=MESH,
        )

    def z_arrival(i):
        t = lax.rem(r - 2 * i + n_rows, n_rows)
        return pltpu.make_async_remote_copy(
            gath.at[t], gath.at[t], gz_ss.at[i], gz_rs.at[i], device_id=(t, s), device_id_type=MESH
        )

    def x_copy(i):
        t = lax.rem(r - 2 * i + n_rows, n_rows)
        return pltpu.make_async_remote_copy(
            gath.at[t], gath.at[t], gx_ss.at[i], gx_rs.at[i], device_id=(r1, s), device_id_type=MESH
        )

    def x_arrival(i):
        t = lax.rem(r1 - 2 * i + n_rows, n_rows)
        return pltpu.make_async_remote_copy(
            gath.at[t], gath.at[t], gx_ss.at[i], gx_rs.at[i], device_id=(r1, s), device_id_type=MESH
        )

    def store(b, i):
        rows = pl.ds(pl.multiple_of(lax.rem(b, nbh) * h, h), h)
        cols = pl.ds(pl.multiple_of(lax.div(b, nbh) * w, w), w)
        return pltpu.make_async_copy(gath.at[b], out_hbm.at[rows, cols], out_sem.at[i])

    over(1, half, lambda i: z_copy(i).start())
    x_copy(0).start()
    store(r, 0).start()

    def forward(i):
        z_arrival(i).wait_recv()
        x_copy(i).start()
        store(lax.rem(r - 2 * i + n_rows, n_rows), i).start()

    over(1, half, forward)

    def keep(i):
        x_arrival(i).wait_recv()
        store(lax.rem(r1 - 2 * i + n_rows, n_rows), half + i).start()

    over(0, half, keep)

    over(0, n_ct, lambda j: core_copy(j).wait_send())
    over(0, n_rows, lambda m: y_copy(m).wait_send())

    def sent(m):
        @pl.when(block_of(m) != r)
        def _():
            r_copy(m).wait_send()

    over(0, n_rows, sent)
    over(1, half, lambda i: z_copy(i).wait_send())
    over(0, half, lambda i: x_copy(i).wait_send())
    over(0, half, lambda i: store(lax.rem(r - 2 * i + n_rows, n_rows), i).wait())
    over(0, half, lambda i: store(lax.rem(r1 - 2 * i + n_rows, n_rows), half + i).wait())


def per_device(n_rows, n_sub, documents, centroids, cluster_mass):
    n_docs, d = documents.shape
    k = centroids.shape[0]
    slab = k // n_sub
    n_ct = d // TILE
    w = LANES
    h = slab * d // (w * n_rows)
    dma = pltpu.SemaphoreType.DMA
    vm = pltpu.VMEM
    blocks = (n_rows, h, w)
    out, duals = pl.pallas_call(
        functools.partial(kernel, n_rows, n_sub),
        out_shape=(
            jax.ShapeDtypeStruct((slab, d), BF16),
            jax.ShapeDtypeStruct((k // LANES, LANES), F32),
        ),
        in_specs=[
            pl.BlockSpec(memory_space=pl.ANY),
            pl.BlockSpec(memory_space=pl.ANY),
            pl.BlockSpec(memory_space=pl.ANY),
        ],
        out_specs=(pl.BlockSpec(memory_space=pl.ANY), pl.BlockSpec(memory_space=pltpu.VMEM)),
        scratch_shapes=[
            vm((n_docs, d), BF16), vm((k, d), BF16), vm((k, n_docs), F32), vm((k, n_docs), BF16),
            vm((k, LANES), F32), vm((k, LANES), F32),
            vm((k // LANES, LANES), F32), vm((k // LANES, LANES), F32), vm((k // LANES, LANES), F32), vm((1, LANES), F32), vm((1, n_docs), F32),
            vm((ITERS, n_sub, k // LANES, LANES), F32), vm((ITERS, n_rows, k // LANES, LANES), F32),
            vm((n_ct, 2 * slab, TILE), F32), vm((n_ct, 2 * slab, TILE), F32),
            vm(blocks, F32), vm(blocks, BF16), vm(blocks, BF16), vm(blocks, BF16), vm(blocks, BF16), vm(blocks, BF16),
            dma((n_sub + n_docs // TILE + 1,)), dma((n_rows,)),
            dma((ITERS, 3)), dma((ITERS, 3)), dma((ITERS, n_rows)), dma((ITERS, n_rows)),
            dma((n_ct,)), dma((n_ct,)), dma((n_rows,)), dma((n_rows,)), dma((n_rows,)), dma((n_rows,)),
            dma((n_rows // 2,)), dma((n_rows // 2,)), dma((n_rows // 2,)), dma((n_rows // 2,)),
        ],
        compiler_params=pltpu.CompilerParams(
            collective_id=0, has_side_effects=True, vmem_limit_bytes=52 * 1024 * 1024
        ),
        cost_estimate=pl.CostEstimate(
            flops=4 * n_docs * k * d, bytes_accessed=2 * (n_docs * d + k * d + slab * d),
            transcendentals=2 * ITERS * n_docs * k,
        ),
    )(documents, centroids, cluster_mass.reshape(k // LANES, LANES))
    return out, duals.reshape(k)


def solution(mesh):
    return jax.shard_map(
        functools.partial(per_device, mesh.shape["rows"], mesh.shape["sub"]),
        mesh=mesh,
        in_specs=(P(("rows", "sub"), None), P(), P()),
        out_specs=(P("sub", None), P()),
        check_vma=False,
    )
```

```python
import functools
import math

import jax
import jax.numpy as jnp
from jax import lax
from jax.experimental import pallas as pl
from jax.experimental.pallas import tpu as pltpu
from jax.sharding import PartitionSpec as P

ITERS = 3
TAU = 0.8
TEMP = 4.0
LOG2E = math.log2(math.e)
HEADROOM = 112.0
LANES = 128
TILE = 256
F32, BF16 = jnp.float32, jnp.bfloat16
MESH = pl.DeviceIdType.MESH


def kernel(n_rows, n_sub, docs_hbm, cent_hbm, cmass_hbm, out_hbm, duals_ref,
           docs, cent, scores, plan, dual_b, acc, col, cmass, shifted, adjust, lse, p1, p2, core_s, core_r, own, away, e_s, e_r, y_s, y_r, r_s, r_r, gath,
           in_sem, out_sem, p1_ss, p1_rs, p2_ss, p2_rs, c_ss, c_rs, e_ss, e_rs, y_ss, y_rs, r_ss, r_rs, gz_ss, gz_rs, gx_ss, gx_rs):
    n_docs, d = docs.shape
    k_all = cent.shape[0]
    slab = k_all // n_sub
    rps = slab // LANES
    h, w = own.shape[1:]
    nbh = slab // h
    n_ct = d // TILE
    bpc = n_rows // n_ct
    r, s = lax.axis_index("rows"), lax.axis_index("sub")
    s1 = s + 1 - 2 * lax.rem(s, 2)
    s2 = lax.rem(s + 2, n_sub)
    s3 = n_sub - 1 - s
    order = (s3, s1, s2, s)
    r1 = r + 1 - 2 * lax.rem(r, 2)

    barrier = pltpu.get_barrier_semaphore()
    for t in (s1, s2, s3):
        pl.semaphore_signal(barrier, inc=1, device_id=(r, t), device_id_type=MESH)

    def greet(i, _):
        pl.semaphore_signal(barrier, inc=1, device_id=(lax.rem(r + i, n_rows), s), device_id_type=MESH)
        return 0

    lax.fori_loop(1, n_rows, greet, 0)

    def cent_copy(l):
        rows = pl.ds(pl.multiple_of(order[l] * slab, slab), slab)
        return pltpu.make_async_copy(cent_hbm.at[rows, :], cent.at[pl.ds(l * slab, slab), :], in_sem.at[l])

    def docs_copy(c):
        rows = pl.ds(pl.multiple_of(c * TILE, TILE), TILE)
        return pltpu.make_async_copy(docs_hbm.at[rows, :], docs.at[rows, :], in_sem.at[n_sub + c])

    n_chunks = n_docs // TILE
    docs_copy(0).start()
    for l in range(n_sub):
        cent_copy(l).start()
    for c in range(1, n_chunks):
        docs_copy(c).start()
    cmass_copy = pltpu.make_async_copy(cmass_hbm, cmass, in_sem.at[n_sub + n_chunks])
    cmass_copy.start()
    for l in range(n_sub):
        cent_copy(l).wait()
    cmass_copy.wait()

    scale = TEMP / math.sqrt(d) * LOG2E
    loga = -math.log2(n_docs * n_rows * n_sub)
    parts = 8
    size = k_all // parts
    slices = [pl.ds(q * size, size) for q in range(parts)]

    def halves(c):
        return [pl.ds(pl.multiple_of(c * TILE + u * LANES, LANES), LANES) for u in range(TILE // LANES)]

    def eight(value, axis_op):
        return axis_op(value.reshape(size // 8, 8, LANES), axis=0)

    def tree(values, op, axis_op):
        while len(values) > 1:
            values = [op(a, b) for a, b in zip(values[::2], values[1::2])]
        return axis_op(values[0], axis=0, keepdims=True)

    def mass_slice(keep, ks, cols, row_duals):
        masses = [jnp.exp2(scores[ks, cu] + rd) for cu, rd in zip(cols, row_duals)]
        acc[ks, :] += sum(masses[1:], masses[0])
        if keep:
            for cu, mass in zip(cols, masses):
                plan[ks, cu] = mass.astype(BF16)

    def step(initial, following, current, row_duals):
        sums = None
        if following is not None:
            cols = halves(following)
            if initial:
                shift = [
                    tree([eight(scores[ks, cu], jnp.max) for ks in slices], jnp.maximum, jnp.max) for cu in cols
                ]
            else:
                shift = [lse[:, cu] for cu in cols]
            sums = [[] for _ in cols]
        for ks in slices:
            if following is not None:
                for cu, top, out in zip(cols, shift, sums):
                    x = scores[ks, cu] if initial else scores[ks, cu] + dual_b[ks, :]
                    out.append(eight(jnp.exp2(x - top), jnp.sum))
            if current is not None:
                mass_slice(True, ks, halves(current), row_duals)
        if following is None:
            return None
        result = []
        for cu, top, values in zip(cols, shift, sums):
            value = top + jnp.log(tree(values, jnp.add, jnp.sum)) * LOG2E
            if not initial:
                value = value + adjust[...]
            lse[:, cu] = value
            result.append(TAU * (loga - value))
        return tuple(result)

    def first_chunk(c):
        docs_copy(c).wait()
        rows = pl.ds(pl.multiple_of(c * TILE, TILE), TILE)
        scores[:, rows] = lax.dot_general(
            cent[...], docs[rows, :], (((1,), (1,)), ((), ())), preferred_element_type=F32
        ) * scale
        row_duals = step(True, c, None, None)
        for ks in slices:
            mass_slice(False, ks, halves(c), row_duals)

    def later_pass():
        row_duals = step(False, 0, None, None)
        row_duals = lax.fori_loop(0, n_chunks - 1, lambda c, rd: step(False, c + 1, c, rd), row_duals)
        step(False, None, n_chunks - 1, row_duals)

    def p1_copy(it, i):
        t = (s1, s2, s3)[i]
        return pltpu.make_async_remote_copy(
            p1.at[it, s], p1.at[it, s], p1_ss.at[it, i], p1_rs.at[it, i], device_id=(r, t), device_id_type=MESH
        )

    def p1_arrival(it, i):
        t = (s1, s2, s3)[i]
        return pltpu.make_async_remote_copy(
            p1.at[it, t], p1.at[it, t], p1_ss.at[it, i], p1_rs.at[it, i], device_id=(r, t), device_id_type=MESH
        )

    def p2_copy(it, i):
        t = lax.rem(r + i, n_rows)
        return pltpu.make_async_remote_copy(
            p2.at[it, r], p2.at[it, r], p2_ss.at[it, i], p2_rs.at[it, i], device_id=(t, s), device_id_type=MESH
        )

    def p2_arrival(it, i):
        t = lax.rem(r - i + n_rows, n_rows)
        return pltpu.make_async_remote_copy(
            p2.at[it, t], p2.at[it, t], p2_ss.at[it, i], p2_rs.at[it, i], device_id=(t, s), device_id_type=MESH
        )

    def over(start, n, f):
        def body(i, _):
            f(i)
            return 0
        lax.fori_loop(start, n, body, 0)

    def mass_send(it):
        for l in range(n_sub):
            for j in range(rps):
                block = acc[pl.ds(l * slab + j * LANES, LANES), :]
                p1[it, s, pl.ds(order[l] * rps + j, 1), :] = jnp.sum(block.T, axis=0, keepdims=True)
        for i in range(3):
            p1_copy(it, i).start()

    def mass_mid(it):
        for i in range(3):
            p1_arrival(it, i).wait_recv()
        p2[it, r] = (p1[it, 0] + p1[it, 1]) + (p1[it, 2] + p1[it, 3])
        over(1, n_rows, lambda i: p2_copy(it, i).start())

    def spread(value_ref, first_slab):
        for l in range(first_slab, n_sub):
            for j in range(rps):
                row = value_ref[pl.ds(order[l] * rps + j, 1), :]
                dual_b[pl.ds(l * slab + j * LANES, LANES), :] = jnp.broadcast_to(row, (LANES, LANES)).T

    def mass_end(it, last):
        over(1, n_rows, lambda i: p2_arrival(it, i).wait_recv())
        col[...] = lax.fori_loop(1, n_rows, lambda i, a: a + p2[it, i], p2[it, 0])
        new = TAU * (jnp.log(cmass[...]) - jnp.log(col[...]))
        if last:
            spread(col, n_sub - 1)
        else:
            change = LOG2E * (new - duals_ref[...])
            most = jnp.max(jnp.max(change, axis=0, keepdims=True), axis=1, keepdims=True)
            adjust[...] = jnp.broadcast_to(most - HEADROOM, adjust.shape)
            shifted[...] = LOG2E * new - (most - HEADROOM)
            spread(shifted, 0)
        duals_ref[...] = new
        for i in range(3):
            p1_copy(it, i).wait_send()
        over(1, n_rows, lambda i: p2_copy(it, i).wait_send())

    acc[...] = jnp.zeros_like(acc)
    duals_ref[...] = jnp.zeros_like(duals_ref)
    over(0, n_chunks, first_chunk)
    pl.semaphore_wait(barrier, 3 + n_rows - 1)
    mass_send(0)

    def iteration(it):
        mass_mid(it - 1)
        mass_end(it - 1, False)
        acc[...] = jnp.zeros_like(acc)
        later_pass()
        mass_send(it)

    over(1, ITERS, iteration)

    def tile_of(j):
        return lax.rem(lax.div(r, bpc) + 1 + j, n_ct)

    def product(first_row, j):
        cols = pl.ds(pl.multiple_of(tile_of(j) * TILE, TILE), TILE)
        return jnp.dot(plan[pl.ds(first_row, 2 * slab), :], docs[:, cols], preferred_element_type=F32)

    def core_copy(j):
        return pltpu.make_async_remote_copy(
            core_s.at[j], core_r.at[j], c_ss.at[j], c_rs.at[j], device_id=(r, s1), device_id_type=MESH
        )

    def y_copy(m):
        return pltpu.make_async_remote_copy(
            y_s.at[m], y_r.at[m], y_ss.at[m], y_rs.at[m], device_id=(r, s2), device_id_type=MESH
        )

    def far(j):
        core_s[j] = product(0, j)
        core_copy(j).start()

    def near(j):
        both = product(2 * slab, j)
        core_copy(j).wait_recv()
        both = both + core_r[j]
        for q in range(bpc):
            m, i, c = j * bpc + q, (q % nbh) * h, (q // nbh) * w
            away[m] = both[i:i + h, c:c + w]
            own[m] = both[slab + i:slab + i + h, c:c + w]

        @pl.when(j < n_ct // 2)
        def _():
            def pair(p):
                m = j * bpc + 2 * p + 1 - lax.rem(r, 2)
                e_s[m, 0] = away[m].astype(BF16)
                e_s[m, 1] = own[m].astype(BF16)
                e_copy(m).start()
            over(0, bpc // 2, pair)

        @pl.when(j >= n_ct // 2)
        def _():
            over(j * bpc, (j + 1) * bpc, y_send)

    def e_copy(m):
        return pltpu.make_async_remote_copy(
            e_s.at[m], e_r.at[m], e_ss.at[m], e_rs.at[m], device_id=(r1, s), device_id_type=MESH
        )

    def y_send(m):
        y_s[m] = away[m].astype(BF16)
        y_copy(m).start()

    early = n_rows // 2
    pairs = early // 2

    def mine_of(p):
        return 2 * p + lax.rem(r, 2)

    def theirs_of(p):
        return 2 * p + 1 - lax.rem(r, 2)

    def e_reduce(p):
        m = mine_of(p)
        pltpu.make_async_remote_copy(
            e_r.at[m], e_r.at[m], e_ss.at[m], e_rs.at[m], device_id=(r1, s), device_id_type=MESH
        ).wait_recv()
        away[m] = away[m] + e_r[m, 0].astype(F32)
        own[m] = own[m] + e_r[m, 1].astype(F32)
        y_send(m)

    over(0, n_ct, far)
    mass_mid(ITERS - 1)
    over(0, n_ct, near)
    over(0, pairs, e_reduce)

    def block_of(m):
        return tile_of(lax.div(m, bpc)) * bpc + lax.rem(m, bpc)

    def r_copy(m):
        b = block_of(m)
        return pltpu.make_async_remote_copy(
            r_s.at[m], r_r.at[r], r_ss.at[m], r_rs.at[r], device_id=(b, s), device_id_type=MESH
        )

    def r_arrival(t):
        return pltpu.make_async_remote_copy(
            r_r.at[t], r_r.at[t], r_ss.at[0], r_rs.at[t], device_id=(t, s), device_id_type=MESH
        )

    def reduce_block(m):
        y_copy(m).wait_recv()
        own[m] = own[m] + y_r[m].astype(F32)

        @pl.when(block_of(m) != r)
        def _():
            r_s[m] = own[m].astype(BF16)
            r_copy(m).start()

    over(0, pairs, lambda p: reduce_block(mine_of(p)))
    over(early, n_rows, reduce_block)
    mass_end(ITERS - 1, True)

    final = n_rows - bpc + lax.rem(r, bpc)

    def gather_sum(i, _):
        t = lax.rem(r - i + n_rows, n_rows)
        place = lax.rem(lax.div(r, bpc) - lax.div(t, bpc) - 1 + 2 * n_ct, n_ct)
        expected = lax.rem(lax.rem(i, 2) * (1 - lax.div(2 * place, n_ct)), 2) == 0

        @pl.when(expected)
        def _():
            r_arrival(t).wait_recv()
            own[final] = own[final] + r_r[t].astype(F32)
        return 0

    lax.fori_loop(1, n_rows, gather_sum, 0)
    total = own[final]
    i0 = pl.multiple_of((n_sub - 1) * slab + lax.rem(r, nbh) * h, h)
    gath[r] = (total / dual_b[pl.ds(i0, h), :]).astype(BF16)

    half = n_rows // 2

    def z_copy(i):
        return pltpu.make_async_remote_copy(
            gath.at[r], gath.at[r], gz_ss.at[i], gz_rs.at[i],
            device_id=(lax.rem(r + 2 * i, n_rows), s), device_id_type=MESH,
        )

    def z_arrival(i):
        t = lax.rem(r - 2 * i + n_rows, n_rows)
        return pltpu.make_async_remote_copy(
            gath.at[t], gath.at[t], gz_ss.at[i], gz_rs.at[i], device_id=(t, s), device_id_type=MESH
        )

    def x_copy(i):
        t = lax.rem(r - 2 * i + n_rows, n_rows)
        return pltpu.make_async_remote_copy(
            gath.at[t], gath.at[t], gx_ss.at[i], gx_rs.at[i], device_id=(r1, s), device_id_type=MESH
        )

    def x_arrival(i):
        t = lax.rem(r1 - 2 * i + n_rows, n_rows)
        return pltpu.make_async_remote_copy(
            gath.at[t], gath.at[t], gx_ss.at[i], gx_rs.at[i], device_id=(r1, s), device_id_type=MESH
        )

    def store(b, i):
        rows = pl.ds(pl.multiple_of(lax.rem(b, nbh) * h, h), h)
        cols = pl.ds(pl.multiple_of(lax.div(b, nbh) * w, w), w)
        return pltpu.make_async_copy(gath.at[b], out_hbm.at[rows, cols], out_sem.at[i])

    over(1, half, lambda i: z_copy(i).start())
    x_copy(0).start()
    store(r, 0).start()

    def forward(i):
        z_arrival(i).wait_recv()
        x_copy(i).start()
        store(lax.rem(r - 2 * i + n_rows, n_rows), i).start()

    over(1, half, forward)

    def keep(i):
        x_arrival(i).wait_recv()
        store(lax.rem(r1 - 2 * i + n_rows, n_rows), half + i).start()

    over(0, half, keep)

    over(0, n_ct, lambda j: core_copy(j).wait_send())
    over(0, pairs, lambda p: e_copy(theirs_of(p)).wait_send())
    over(0, pairs, lambda p: y_copy(mine_of(p)).wait_send())
    over(early, n_rows, lambda m: y_copy(m).wait_send())

    def sent(m):
        @pl.when(block_of(m) != r)
        def _():
            r_copy(m).wait_send()

    over(0, pairs, lambda p: sent(mine_of(p)))
    over(early, n_rows, sent)
    over(1, half, lambda i: z_copy(i).wait_send())
    over(0, half, lambda i: x_copy(i).wait_send())
    over(0, half, lambda i: store(lax.rem(r - 2 * i + n_rows, n_rows), i).wait())
    over(0, half, lambda i: store(lax.rem(r1 - 2 * i + n_rows, n_rows), half + i).wait())


def per_device(n_rows, n_sub, documents, centroids, cluster_mass):
    n_docs, d = documents.shape
    k = centroids.shape[0]
    slab = k // n_sub
    n_ct = d // TILE
    w = LANES
    h = slab * d // (w * n_rows)
    dma = pltpu.SemaphoreType.DMA
    vm = pltpu.VMEM
    blocks = (n_rows, h, w)
    out, duals = pl.pallas_call(
        functools.partial(kernel, n_rows, n_sub),
        out_shape=(
            jax.ShapeDtypeStruct((slab, d), BF16),
            jax.ShapeDtypeStruct((k // LANES, LANES), F32),
        ),
        in_specs=[
            pl.BlockSpec(memory_space=pl.ANY),
            pl.BlockSpec(memory_space=pl.ANY),
            pl.BlockSpec(memory_space=pl.ANY),
        ],
        out_specs=(pl.BlockSpec(memory_space=pl.ANY), pl.BlockSpec(memory_space=pltpu.VMEM)),
        scratch_shapes=[
            vm((n_docs, d), BF16), vm((k, d), BF16), vm((k, n_docs), F32), vm((k, n_docs), BF16),
            vm((k, LANES), F32), vm((k, LANES), F32),
            vm((k // LANES, LANES), F32), vm((k // LANES, LANES), F32), vm((k // LANES, LANES), F32), vm((1, LANES), F32), vm((1, n_docs), F32),
            vm((ITERS, n_sub, k // LANES, LANES), F32), vm((ITERS, n_rows, k // LANES, LANES), F32),
            vm((n_ct, 2 * slab, TILE), F32), vm((n_ct, 2 * slab, TILE), F32),
            vm(blocks, F32), vm(blocks, F32), vm((n_rows // 2, 2, h, w), BF16), vm((n_rows // 2, 2, h, w), BF16),
            vm(blocks, BF16), vm(blocks, BF16), vm(blocks, BF16), vm(blocks, BF16), vm(blocks, BF16),
            dma((n_sub + n_docs // TILE + 1,)), dma((n_rows,)),
            dma((ITERS, 3)), dma((ITERS, 3)), dma((ITERS, n_rows)), dma((ITERS, n_rows)),
            dma((n_ct,)), dma((n_ct,)), dma((n_rows // 2,)), dma((n_rows // 2,)), dma((n_rows,)), dma((n_rows,)), dma((n_rows,)), dma((n_rows,)),
            dma((n_rows // 2,)), dma((n_rows // 2,)), dma((n_rows // 2,)), dma((n_rows // 2,)),
        ],
        compiler_params=pltpu.CompilerParams(
            collective_id=0, has_side_effects=True, vmem_limit_bytes=52 * 1024 * 1024
        ),
        cost_estimate=pl.CostEstimate(
            flops=4 * n_docs * k * d, bytes_accessed=2 * (n_docs * d + k * d + slab * d),
            transcendentals=2 * ITERS * n_docs * k,
        ),
    )(documents, centroids, cluster_mass.reshape(k // LANES, LANES))
    return out, duals.reshape(k)


def solution(mesh):
    return jax.shard_map(
        functools.partial(per_device, mesh.shape["rows"], mesh.shape["sub"]),
        mesh=mesh,
        in_specs=(P(("rows", "sub"), None), P(), P()),
        out_specs=(P("sub", None), P()),
        check_vma=False,
    )
```
